32 devices in a mesh: seq: 4 (over z), head: 8 (over y, x, core).
Axes of the slice: x: 2, y: 2, z: 4, core: 2. Of those that a mesh axis runs over, the one named last changes fastest.
Arguments:
- query: bfloat16 [32768, 2048], P('seq', 'head'), may hold values from -4.5 to 4.5
- keys: bfloat16 [32768, 2048], P('seq', 'head'), may hold values from -4.5 to 4.5
- values: bfloat16 [32768, 2048], P('seq', 'head'), may hold values from -6 to 6
- mem_init: float32 [16, 128, 128], P('head'), may hold values from -362.03867 to 362.03867
- beta: float32 [16], P('head'), may hold values from -2 to 2
- mem_gain: float32 [2048], P('head'), may hold values from 0.1 to 1.9
- loc_gain: float32 [2048], P('head'), may hold values from 0.1 to 1.9
- w_out: bfloat16 [2048, 2048], P('head'), may hold values from -0.125 to 0.125
Outputs:
- attn_out: bfloat16 [32768, 2048], P(('seq', 'head'))
- memory_prefix: float32 [4, 16, 128, 128], P('seq', 'head')
The draws below stay inside these ranges and needn't reach their ends.
All inputs are finite; a program needn't handle non-finite values.
Results may differ from the reference program's by a relative error of at most 0.0054.
Values may be sent and summed in bfloat16 or wider, within the bound.
No kernel may reach another device: no remote copies, remote signals or barrier semaphores. Data moves between devices by JAX's collectives and lax.ppermute only.
A program may use at most 128 MiB of HBM per device.

```python
import jax
import jax.numpy as jnp
from jax import lax

H = 16
HD = 128
SEG = 2048
SEGS_DEV = 4
D = 2048
TOK_DEV = 8192
TOKENS = 32768


def drawn_pair(key):
    query_key = jax.random.fold_in(key, 11)
    keys_key = jax.random.fold_in(key, 12)
    query = jnp.clip(jax.random.normal(query_key, (TOKENS, D), jnp.float32), -4.5, 4.5)
    keys = jnp.clip(jax.random.normal(keys_key, (TOKENS, D), jnp.float32), -4.5, 4.5)
    return (query, keys)


def draw_query(key, part):
    return drawn_pair(key)[0].astype(jnp.bfloat16)


def draw_keys(key, part):
    return drawn_pair(key)[1].astype(jnp.bfloat16)


def steps_of(key, extent, cuts, smallest, high):
    factor_of, own = 1.0, jax.random.fold_in(key, 6)
    for position, parts in cuts:
        draws = jnp.exp(jax.random.uniform(jax.random.fold_in(own, position), (parts,), jnp.float32, smallest / len(cuts), high / len(cuts)))
        factor_of = factor_of * jnp.repeat(draws, extent[position] // parts).reshape([-1 if axis == position else 1 for axis in range(len(extent))])
    return factor_of


def noise(key, dims, deviation, most, cuts=(), kind=jnp.bfloat16):
    entries = jax.random.normal(key, dims, jnp.float32) * deviation
    if len(cuts) > 0:
        entries = steps_of(key, dims, cuts, -0.22, 0.18) * entries
    return jnp.clip(entries, min=-most, max=most).astype(kind)


def setup_inputs(seed: int = 0) -> dict:
    key_of = jax.random.split(jax.random.key(seed), 9)
    return {
        "query": draw_query(jax.random.fold_in(key_of[8], 71), 0),
        "keys": draw_keys(jax.random.fold_in(key_of[8], 71), 0),
        "values": noise(key_of[2], (TOKENS, D), 1.0, 6.0, ((0, 4), (1, 8))),
        "mem_init": noise(key_of[3], (H, HD, HD), (TOK_DEV ** 0.5), 362.03867, ((0, 8),), jnp.float32),
        "beta": jnp.clip(jax.random.uniform(key_of[4], (H,), jnp.float32, -2.0, 2.0) * steps_of(key_of[4], (H,), ((0, 8),), -0.4, 0.0), -2.0, 2.0),
        "mem_gain": jnp.clip(1.0 + 0.18 * jax.random.normal(key_of[5], (D,), jnp.float32), 0.1, 1.9),
        "loc_gain": jnp.clip(1.0 + 0.18 * jax.random.normal(key_of[6], (D,), jnp.float32), 0.1, 1.9),
        "w_out": noise(key_of[7], (D, D), D ** -0.5, 0.125, ((0, 8),)),
    }


def elu_feature(source):
    return (jax.nn.elu(source.astype(jnp.float32)) + 1.0).astype(jnp.bfloat16)

def rms_norm(source, gain_vec):
    mean_sq = lax.optimization_barrier(jnp.mean(source * source, axis=-1, keepdims=True))
    return source * lax.rsqrt(mean_sq + 1e-06) * gain_vec

def segment_attention(q_seg, k_seg, v_seg):
    length = q_seg.shape[0]
    scores = jnp.dot(q_seg, k_seg.T, preferred_element_type=jnp.float32) * HD ** (-0.5)
    row_pos = lax.broadcasted_iota(jnp.int32, (length, length), 0)
    col_pos = lax.broadcasted_iota(jnp.int32, (length, length), 1)
    scores = jnp.where(col_pos <= row_pos, scores, -jnp.inf)
    largest = lax.optimization_barrier(jnp.max(scores, axis=-1, keepdims=True))
    weights = jnp.exp(scores - largest)
    denominator = lax.optimization_barrier(jnp.sum(weights, axis=-1, keepdims=True))
    probabilities = (weights / denominator).astype(jnp.bfloat16)
    return jnp.dot(probabilities, v_seg, preferred_element_type=jnp.float32)

def reference(query, keys, values, mem_init, beta, mem_gain, loc_gain, w_out):
    seg_total = TOKENS // SEG

    def one_head(head_pos):

        def column(source):
            return lax.dynamic_slice_in_dim(source, head_pos * HD, HD, 1).reshape(seg_total, SEG, HD)
        q_head = column(query)
        k_head = column(keys)
        v_head = column(values)

        def attend(triple):
            return segment_attention(triple[0], triple[1], triple[2])
        local = lax.map(attend, (q_head, k_head, v_head))
        q_feat = elu_feature(q_head).astype(jnp.float32)
        k_feat = elu_feature(k_head).astype(jnp.float32)
        kv_terms = jnp.einsum('nsa,nsb->nab', k_feat, v_head.astype(jnp.float32), precision=lax.Precision.HIGHEST)
        inclusive = jnp.cumsum(kv_terms, axis=0)
        earlier = jnp.concatenate([jnp.zeros((1, HD, HD), jnp.float32), inclusive[:-1]], axis=0)
        memory = mem_init[head_pos] + earlier
        read = jnp.einsum('nsa,nab->nsb', q_feat, memory, precision=lax.Precision.HIGHEST)
        gate_value = jax.nn.sigmoid(beta[head_pos])
        m_gain = lax.dynamic_slice_in_dim(mem_gain, head_pos * HD, HD)
        l_gain = lax.dynamic_slice_in_dim(loc_gain, head_pos * HD, HD)
        mixed = gate_value * rms_norm(read, m_gain) + (1.0 - gate_value) * rms_norm(local, l_gain)
        head_out = mixed.astype(jnp.bfloat16).reshape(TOKENS, HD)
        prefix = memory[::SEGS_DEV] * TOK_DEV ** (-0.5)
        return (head_out, prefix)
    head_outs, prefixes = lax.map(one_head, jnp.arange(H, dtype=jnp.int32))
    joined = jnp.transpose(head_outs, (1, 0, 2)).reshape(TOKENS, H * HD)
    attn_out = jnp.dot(joined, w_out, preferred_element_type=jnp.float32).astype(jnp.bfloat16)
    return (attn_out, jnp.transpose(prefixes, (1, 0, 2, 3)))
```

```python
import functools

import jax
import jax.numpy as jnp
from jax import lax
from jax.experimental import pallas as pl
from jax.experimental.pallas import tpu as pltpu
from jax.sharding import PartitionSpec as P

HD = 128
SEG = 2048
BLOCK = 256
EPS = 1e-06
LOG2E = 1.4426950408889634
VMEM = 56 << 20
F32, BF16 = jnp.float32, jnp.bfloat16


def call(body, name, out_shape, grid_spec, flops, bytes_accessed, transcendentals=0):
    return pl.pallas_call(
        body,
        name=name,
        out_shape=out_shape,
        grid_spec=grid_spec,
        compiler_params=pltpu.CompilerParams(vmem_limit_bytes=VMEM),
        cost_estimate=pl.CostEstimate(
            flops=flops, bytes_accessed=bytes_accessed, transcendentals=transcendentals
        ),
    )


def whole(shape, memory_space=pltpu.VMEM):
    return pl.BlockSpec(shape, lambda *_: (0,) * len(shape), memory_space=memory_space)


def elu_feature(source):
    wide = source.astype(F32)
    return jnp.where(wide > 0, wide + 1.0, jnp.exp(wide)).astype(BF16)


def columns(head):
    return slice(head * HD, (head + 1) * HD)


def kv_body(k_ref, v_ref, term_ref, total_ref):
    for head in range(k_ref.shape[1] // HD):
        cols = columns(head)
        term = lax.dot_general(
            elu_feature(k_ref[:, cols]),
            v_ref[:, cols],
            (((0,), (0,)), ((), ())),
            preferred_element_type=F32,
        )
        term_ref[0, head] = term

        @pl.when(pl.program_id(0) == 0)
        def _():
            total_ref[head] = term

        @pl.when(pl.program_id(0) > 0)
        def _():
            total_ref[head] += term


def kv_terms(keys, values):
    tokens, width = keys.shape
    heads, segs = width // HD, tokens // SEG
    block = pl.BlockSpec((SEG, width), lambda seg: (seg, 0))
    return call(
        kv_body,
        "kv_terms",
        (
            jax.ShapeDtypeStruct((segs, heads, HD, HD), F32),
            jax.ShapeDtypeStruct((heads, HD, HD), F32),
        ),
        pl.GridSpec(
            grid=(segs,),
            in_specs=[block, block],
            out_specs=[
                pl.BlockSpec((1, heads, HD, HD), lambda seg: (seg, 0, 0, 0)),
                pl.BlockSpec((heads, HD, HD), lambda seg: (0, 0, 0)),
            ],
        ),
        2 * tokens * width * HD,
        2 * keys.size * 2,
    )(keys, values)


def mean_square(source):
    return jnp.mean(source * source, axis=-1, keepdims=True)


def local_branch(q, k, v, scale_gain):
    rows, end = q.shape[0], k.shape[0]
    wide = q.astype(F32) * (HD**-0.5 * LOG2E)
    high = wide.astype(BF16)
    low = (wide - high.astype(F32)).astype(BF16)
    scores = lax.dot_general(
        jnp.concatenate([high, low], axis=1),
        jnp.concatenate([k, k], axis=1),
        (((1,), (1,)), ((), ())),
        preferred_element_type=F32,
    )
    row = lax.broadcasted_iota(jnp.int32, (rows, rows), 0)
    col = lax.broadcasted_iota(jnp.int32, (rows, rows), 1)
    diagonal = jnp.where(col <= row, scores[:, end - rows :], -jnp.inf)
    if end > rows:
        scores = jnp.concatenate([scores[:, : end - rows], diagonal], axis=1)
    else:
        scores = diagonal
    largest = jnp.max(scores, axis=-1, keepdims=True)
    weights = jnp.exp2(scores - largest).astype(BF16)
    summed = jnp.dot(
        weights, jnp.concatenate([v, jnp.ones_like(v)], axis=1), preferred_element_type=F32
    )
    local, denominator = summed[:, :HD], summed[:, HD:]
    return local * (
        lax.rsqrt(mean_square(local) + EPS * denominator * denominator) * scale_gain
    )


def memory_branch(q, memory_pair, scale_gain):
    both = jnp.dot(elu_feature(q), memory_pair, preferred_element_type=F32)
    read = both[:, :HD] + both[:, HD:]
    return read * (lax.rsqrt(mean_square(read) + EPS) * scale_gain)


def memory_pair_of(seg, head, base_ref, term_ref):
    memory = base_ref[head]
    for earlier in range(term_ref.shape[0] - 1):
        memory = memory + jnp.where(earlier < seg, term_ref[earlier, head], 0.0)
    high = memory.astype(BF16)
    low = (memory - high.astype(F32)).astype(BF16)
    return jnp.concatenate([high, low], axis=1)


def gate_of(beta_ref, head):
    return 1.0 / (1.0 + jnp.exp(-jnp.full((1, HD), beta_ref[head], F32)))


def local_body(lap, place_ref, q_ref, k_ref, v_ref, beta_ref, gain_ref, out_ref):
    for start in range(0, SEG, BLOCK):
        rows, end = slice(start, start + BLOCK), start + BLOCK
        for head in range(q_ref.shape[1] // HD):
            cols = columns(head)
            scale_gain = (1.0 - gate_of(beta_ref, head)) * gain_ref[:, cols]
            out_ref[rows, cols] = local_branch(
                q_ref[rows, cols], k_ref[:end, cols], v_ref[:end, cols], scale_gain
            )


def mix_body(
    lap, place_ref, q_ref, local_ref, base_ref, term_ref, beta_ref, gain_ref, *rest
):
    *out_refs, held = rest
    seg = place_ref[0] ^ lap
    for head in range(q_ref.shape[1] // HD):
        cols = columns(head)
        pair = memory_pair_of(seg, head, base_ref, term_ref)
        scale_gain = gate_of(beta_ref, head) * gain_ref[:, cols]
        for start in range(0, SEG, BLOCK):
            rows = slice(start, start + BLOCK)
            mixed = memory_branch(q_ref[rows, cols], pair, scale_gain) + local_ref[rows, cols]
            held[rows, cols] = mixed.astype(BF16)
    hand_out(place_ref, held, out_refs)


def both_body(
    lap, place_ref, q_ref, k_ref, v_ref, base_ref, term_ref, beta_ref, mem_gain_ref, loc_gain_ref, *rest
):
    *out_refs, held = rest
    seg = place_ref[0] ^ lap
    heads = q_ref.shape[1] // HD
    pairs = [memory_pair_of(seg, head, base_ref, term_ref) for head in range(heads)]
    for start in range(0, SEG, BLOCK):
        rows, end = slice(start, start + BLOCK), start + BLOCK
        for head in range(heads):
            cols = columns(head)
            gate = gate_of(beta_ref, head)
            q = q_ref[rows, cols]
            local = local_branch(
                q, k_ref[:end, cols], v_ref[:end, cols], (1.0 - gate) * loc_gain_ref[:, cols]
            )
            read = memory_branch(q, pairs[head], gate * mem_gain_ref[:, cols])
            held[rows, cols] = (read + local).astype(BF16)
    hand_out(place_ref, held, out_refs)


def hand_out(place_ref, held, out_refs):
    size = out_refs[0].shape[0]
    for turn, out_ref in enumerate(out_refs):
        first = pl.multiple_of((place_ref[1] ^ turn) * size, size)
        out_ref[...] = held[pl.ds(first, size), :]


def attention_cost(width):
    heads = width // HD
    return dict(
        flops=heads * 6 * SEG * SEG * HD,
        bytes_accessed=8 * SEG * width,
        transcendentals=heads * SEG * SEG,
    )


def segment_call(lap, kind, place, arrays, width, dests):
    seg_block = pl.BlockSpec((SEG, width), lambda _, place_ref: (place_ref[0] ^ lap, 0))
    specs = []
    for array in arrays:
        if array.ndim == 2 and array.shape[0] > SEG:
            specs.append(seg_block)
        elif array.ndim == 1:
            specs.append(pl.BlockSpec(memory_space=pltpu.SMEM))
        else:
            specs.append(whole(array.shape))
    if kind == "local":
        out_shape = [jax.ShapeDtypeStruct((SEG, width), F32)]
        scratch = []
    else:
        out_shape = [jax.ShapeDtypeStruct((SEG // dests, width), BF16)] * dests
        scratch = [pltpu.VMEM((SEG, width), BF16)]
    body = {"local": local_body, "mix": mix_body, "both": both_body}[kind]
    cost = attention_cost(width)
    if kind == "mix":
        cost = dict(flops=4 * SEG * width * HD, bytes_accessed=8 * SEG * width)
    return call(
        functools.partial(body, lap),
        f"attention_{kind}",
        out_shape,
        pltpu.PrefetchScalarGridSpec(
            num_scalar_prefetch=1,
            grid=(1,),
            in_specs=specs,
            out_specs=[whole(shape.shape) for shape in out_shape],
            scratch_shapes=scratch,
        ),
        **cost,
    )(place, *arrays)


def project_body(me_ref, *refs):
    *row_refs, w_ref, out_ref, held = refs
    width = row_refs[0].shape[1]
    for turn, row_ref in enumerate(row_refs):
        first = pl.multiple_of((me_ref[0] ^ turn) * width, width)
        held[:, pl.ds(first, width)] = row_ref[...]
    out_ref[...] = jnp.dot(held[...], w_ref[...], preferred_element_type=F32).astype(BF16)


def project(me, rows, w_all):
    count, width = rows[0].shape
    depth, out_width = w_all.shape
    block = min(BLOCK, count)
    return call(
        project_body,
        "project",
        jax.ShapeDtypeStruct((count, out_width), BF16),
        pltpu.PrefetchScalarGridSpec(
            num_scalar_prefetch=1,
            grid=(count // block,),
            in_specs=[pl.BlockSpec((block, width), lambda at, _: (at, 0))] * len(rows)
            + [whole(w_all.shape)],
            out_specs=pl.BlockSpec((block, out_width), lambda at, _: (at, 0)),
            scratch_shapes=[pltpu.VMEM((block, depth), BF16)],
        ),
        2 * count * depth * out_width,
        2 * (count * depth + depth * out_width + count * out_width),
    )(me, *rows, w_all)


def flip(array, axis, size, turn):
    if turn == 0:
        return array
    return lax.ppermute(array, axis, [(at, at ^ turn) for at in range(size)])


def per_device(
    sizes, query, keys, values, mem_init, beta, mem_gain, loc_gain, w_out
):
    seq_size, head_size = sizes
    tokens, width = query.shape
    segs = tokens // SEG
    dests = head_size // segs
    me = lax.axis_index("head")
    place = jnp.stack([me // dests, me % dests]).astype(jnp.int32)
    mem_gain, loc_gain = mem_gain.reshape(1, width), loc_gain.reshape(1, width)

    w_all = lax.all_gather(w_out, "head", axis=0, tiled=True)
    terms, total = kv_terms(keys, values)
    memory_base = mem_init
    for step in range(1, seq_size):
        memory_base = memory_base + lax.ppermute(
            total, "seq", [(at, at + step) for at in range(seq_size - step)]
        )
    memory_prefix = (memory_base * tokens ** (-0.5))[None]

    arrived = [None] * head_size
    for lap in range(segs - 1, -1, -1):
        run = functools.partial(segment_call, lap, place=place, width=width, dests=dests)
        if lap == segs - 1:
            (local,) = run("local", arrays=[query, keys, values, beta, loc_gain])
            parts = run("mix", arrays=[query, local, memory_base, terms, beta, mem_gain])
        else:
            parts = run(
                "both",
                arrays=[query, keys, values, memory_base, terms, beta, mem_gain, loc_gain],
            )
        for turn, part in enumerate(parts):
            arrived[lap * dests + turn] = flip(part, "head", head_size, lap * dests + turn)
    attn_out = project(me.reshape(1).astype(jnp.int32), arrived, w_all)
    return attn_out, memory_prefix


def solution(mesh):
    sizes = (mesh.shape["seq"], mesh.shape["head"])
    in_specs = (
        P("seq", "head"),
        P("seq", "head"),
        P("seq", "head"),
        P("head", None, None),
        P("head"),
        P("head"),
        P("head"),
        P("head", None),
    )
    out_specs = (P(("seq", "head"), None), P("seq", "head", None, None))
    return jax.shard_map(
        functools.partial(per_device, sizes),
        mesh=mesh,
        in_specs=in_specs,
        out_specs=out_specs,
        check_vma=False,
    )
```

```python
import functools

import jax
import jax.numpy as jnp
from jax import lax
from jax.experimental import pallas as pl
from jax.experimental.pallas import tpu as pltpu
from jax.sharding import PartitionSpec as P

HD = 128
SEG = 2048
BLOCK = 256
EPS = 1e-06
LOG2E = 1.4426950408889634
VMEM = 60 << 20
F32, BF16 = jnp.float32, jnp.bfloat16


def call(body, name, out_shape, grid_spec, flops, bytes_accessed, transcendentals=0):
    return pl.pallas_call(
        body,
        name=name,
        out_shape=out_shape,
        grid_spec=grid_spec,
        compiler_params=pltpu.CompilerParams(vmem_limit_bytes=VMEM),
        cost_estimate=pl.CostEstimate(
            flops=flops, bytes_accessed=bytes_accessed, transcendentals=transcendentals
        ),
    )


def whole(shape, memory_space=pltpu.VMEM):
    return pl.BlockSpec(shape, lambda *_: (0,) * len(shape), memory_space=memory_space)


def elu_feature(source):
    wide = source.astype(F32)
    return jnp.where(wide > 0, wide + 1.0, jnp.exp(wide)).astype(BF16)


def columns(head):
    return slice(head * HD, (head + 1) * HD)


def kv_body(k_ref, v_ref, term_ref, total_ref):
    for head in range(k_ref.shape[1] // HD):
        cols = columns(head)
        term = lax.dot_general(
            elu_feature(k_ref[:, cols]),
            v_ref[:, cols],
            (((0,), (0,)), ((), ())),
            preferred_element_type=F32,
        )
        term_ref[0, head] = term

        total_ref[head] = jnp.where(pl.program_id(0) == 0, 0.0, total_ref[head]) + term


def kv_terms(keys, values):
    tokens, width = keys.shape
    heads, segs = width // HD, tokens // SEG
    block = pl.BlockSpec((SEG, width), lambda seg: (seg, 0))
    return call(
        kv_body,
        "kv_terms",
        (
            jax.ShapeDtypeStruct((segs, heads, HD, HD), F32),
            jax.ShapeDtypeStruct((heads, HD, HD), F32),
        ),
        pl.GridSpec(
            grid=(segs,),
            in_specs=[block, block],
            out_specs=[
                pl.BlockSpec((1, heads, HD, HD), lambda seg: (seg, 0, 0, 0)),
                whole((heads, HD, HD)),
            ],
        ),
        2 * tokens * width * HD,
        2 * keys.size * 2,
    )(keys, values)


def mean_square(source):
    return jnp.mean(source * source, axis=-1, keepdims=True)


def scores_of(q, k):
    rows, end = q.shape[0], k.shape[0]
    wide = q.astype(F32) * (HD**-0.5 * LOG2E)
    high = wide.astype(BF16)
    low = (wide - high.astype(F32)).astype(BF16)
    scores = lax.dot_general(
        jnp.concatenate([high, low], axis=1),
        jnp.concatenate([k, k], axis=1),
        (((1,), (1,)), ((), ())),
        preferred_element_type=F32,
    )
    row = lax.broadcasted_iota(jnp.int32, (rows, rows), 0)
    col = lax.broadcasted_iota(jnp.int32, (rows, rows), 1)
    diagonal = jnp.where(col <= row, scores[:, end - rows :], -jnp.inf)
    if end > rows:
        return jnp.concatenate([scores[:, : end - rows], diagonal], axis=1)
    return diagonal


def local_branch(scores, v, scale_gain):
    largest = jnp.max(scores, axis=-1, keepdims=True)
    weights = jnp.exp2(scores - largest).astype(BF16)
    summed = jnp.dot(
        weights, jnp.concatenate([v, jnp.ones_like(v)], axis=1), preferred_element_type=F32
    )
    local, denominator = summed[:, :HD], summed[:, HD:]
    return local * (
        lax.rsqrt(mean_square(local) + EPS * denominator * denominator) * scale_gain
    )


def score_ahead(units, q_ref, k_ref, use):
    def make(unit):
        dest, at, _, end, head = unit
        return scores_of(q_ref[0, dest, at, :, columns(head)], k_ref[:end, columns(head)])

    ahead = make(units[0])
    for unit, following in zip(units, [*units[1:], None]):
        scores = ahead
        if following is not None:
            ahead = make(following)
        use(unit, scores)


def memory_branch(q, memory_pair, scale_gain):
    both = jnp.dot(elu_feature(q), memory_pair, preferred_element_type=F32)
    read = both[:, :HD] + both[:, HD:]
    return read * (lax.rsqrt(mean_square(read) + EPS) * scale_gain)


def gate_of(beta_ref, head):
    return 1.0 / (1.0 + jnp.exp(-jnp.full((1, HD), beta_ref[head], F32)))


def chunk_blocks(dests, blocks, per_dest):
    for dest in range(dests):
        for at, block in enumerate(blocks):
            start = (dest * per_dest + block) * BLOCK
            yield dest, at, slice(at * BLOCK, (at + 1) * BLOCK), start + BLOCK


def units_of(dests, blocks, per_dest, heads):
    return [
        (*found, head) for found in chunk_blocks(dests, blocks, per_dest) for head in range(heads)
    ]


def local_body(blocks, per_dest, q_ref, k_ref, v_ref, beta_ref, gain_ref, out_ref):
    _, dests, _, _, width = q_ref.shape

    def use(unit, scores):
        dest, _, rows, end, head = unit
        cols = columns(head)
        out_ref[dest, rows, cols] = local_branch(
            scores, v_ref[:end, cols], (1.0 - gate_of(beta_ref, head)) * gain_ref[:, cols]
        )

    score_ahead(units_of(dests, blocks, per_dest, width // HD), q_ref, k_ref, use)


def advance_memory(base_ref, term_ref, memory):
    @pl.when(pl.program_id(0) == 0)
    def _():
        memory[...] = base_ref[...]

    pairs = []
    for head in range(memory.shape[0]):
        now = memory[head]
        high = now.astype(BF16)
        low = (now - high.astype(F32)).astype(BF16)
        pairs.append(jnp.concatenate([high, low], axis=1))
        memory[head] = now + term_ref[0, head]
    return pairs


def mix_body(blocks, per_dest, q_ref, local_ref, base_ref, term_ref, beta_ref, gain_ref, out_ref, memory):
    _, dests, _, _, width = q_ref.shape
    pairs = advance_memory(base_ref, term_ref, memory)
    for dest, at, rows, _ in chunk_blocks(dests, blocks, per_dest):
        for head, pair in enumerate(pairs):
            cols = columns(head)
            read = memory_branch(
                q_ref[0, dest, at, :, cols], pair, gate_of(beta_ref, head) * gain_ref[:, cols]
            )
            out_ref[dest, rows, cols] = (read + local_ref[dest, rows, cols]).astype(BF16)


def both_body(
    blocks,
    per_dest,
    q_ref,
    k_ref,
    v_ref,
    base_ref,
    term_ref,
    beta_ref,
    mem_gain_ref,
    loc_gain_ref,
    *rest,
):
    *_, out_ref, memory = rest
    _, dests, _, _, width = q_ref.shape
    pairs = advance_memory(base_ref, term_ref, memory)

    def use(unit, scores):
        dest, at, rows, end, head = unit
        cols = columns(head)
        gate = gate_of(beta_ref, head)
        local = local_branch(scores, v_ref[:end, cols], (1.0 - gate) * loc_gain_ref[:, cols])
        read = memory_branch(q_ref[0, dest, at, :, cols], pairs[head], gate * mem_gain_ref[:, cols])
        out_ref[dest, rows, cols] = (read + local).astype(BF16)

    score_ahead(units_of(dests, blocks, per_dest, width // HD), q_ref, k_ref, use)


def chunk_call(kind, blocks, dests, query, arrays, after=()):
    tokens, width = query.shape
    segs, heads = tokens // SEG, width // HD
    per_dest = SEG // dests // BLOCK
    size = len(blocks) * BLOCK
    q = query.reshape(segs, dests, per_dest, BLOCK, width)
    specs = [
        pl.BlockSpec(
            (pl.Element(1), pl.Element(dests), pl.Element(len(blocks)), pl.Element(BLOCK), pl.Element(width)),
            lambda seg: (seg, 0, blocks[0], 0, 0),
        )
    ]
    for array in arrays:
        if array.shape == query.shape:
            specs.append(pl.BlockSpec((SEG, width), lambda seg: (seg, 0)))
        elif array.ndim == 1:
            specs.append(pl.BlockSpec(memory_space=pltpu.SMEM))
        elif array.ndim == 4:
            specs.append(pl.BlockSpec((1, heads, HD, HD), lambda seg: (seg, 0, 0, 0)))
        elif array.shape[1:] == (size, width):
            specs.append(pl.BlockSpec((dests, size, width), lambda seg: (seg, 0, 0)))
        else:
            specs.append(whole(array.shape))
    specs.extend([pl.BlockSpec(memory_space=pl.ANY)] * len(after))
    body = {"local": local_body, "mix": mix_body, "both": both_body}[kind]
    keys_met = segs * sum(end for *_, end in chunk_blocks(dests, blocks, per_dest))
    cost = dict(
        flops=8 * keys_met * BLOCK * width, bytes_accessed=6 * tokens * width, transcendentals=keys_met * BLOCK * heads
    )
    if kind == "mix":
        cost = dict(flops=8 * segs * dests * size * width * HD, bytes_accessed=8 * segs * dests * size * width)
    return call(
        functools.partial(body, blocks, per_dest),
        f"attention_{kind}",
        jax.ShapeDtypeStruct((segs * dests, size, width), F32 if kind == "local" else BF16),
        pl.GridSpec(
            grid=(segs,),
            in_specs=specs,
            out_specs=pl.BlockSpec((dests, size, width), lambda seg: (seg, 0, 0)),
            scratch_shapes=[] if kind == "local" else [pltpu.VMEM((heads, HD, HD), F32)],
        ),
        **cost,
    )(q, *arrays, *after)


def flip(array, axis, size, turn):
    return lax.ppermute(array, axis, [(at, at ^ turn) for at in range(size)])


class RowGather:
    def __init__(self, w_out, seq_size, head_size):
        half = w_out.shape[0] // 2
        self.seq_size, self.head_size = seq_size, head_size
        self.paired = seq_size % 2 == 0 and half % HD == 0
        own = w_out
        if self.paired:
            own = lax.dynamic_slice_in_dim(w_out, lax.axis_index("seq") % 2 * half, half, 0)
        self.pieces = {0: [w_out]}
        self.own = own

    def near(self):
        for turn in range(2, self.head_size, 2):
            self.pieces[turn] = [flip(self.own, "head", self.head_size, turn)]
        self.across(0)

    def swap(self, turn):
        if self.paired:
            self.pieces[turn].append(flip(self.pieces[turn][0], "seq", self.seq_size, 1))

    def across(self, turn):
        done = self.pieces.setdefault(turn + 1, [])
        for piece in self.pieces[turn][len(done) :]:
            done.append(flip(piece, "head", self.head_size, 1))

    def now(self, *turns):
        return [piece for turn in turns for piece in self.pieces[turn]]

    def all(self):
        return [tuple(self.pieces[turn]) for turn in range(self.head_size)]


def project_body(place_ref, *refs, count, parts_of):
    row_refs, w_refs, out_ref = refs[:count], refs[count : count + sum(parts_of)], refs[-1]
    width = row_refs[0].shape[2]
    rows = []
    for row_ref in row_refs:
        found = []
        for turn, parts in enumerate(parts_of):
            source, size = place_ref[0] ^ turn, width // parts
            for part in range(parts):
                place = part if parts == 1 else place_ref[1] ^ part
                cols = pl.ds(pl.multiple_of(place * size, size), size)
                found.append(row_ref[source, :, cols])
        rows.append(jnp.concatenate(found, axis=1))
    w_all = jnp.concatenate([w_ref[...] for w_ref in w_refs], axis=0)
    out_ref[...] = jnp.dot(
        jnp.concatenate(rows, axis=0), w_all, preferred_element_type=F32
    ).astype(BF16)


def project(place, chunks, pieces, first, tokens, so_far=None):
    sources, _, width = chunks[0].shape
    count = sum(chunk.shape[1] for chunk in chunks)
    flat, parts_of = [], []
    for piece in pieces:
        parts = piece if isinstance(piece, tuple) else (piece,)
        flat.extend(parts)
        parts_of.append(len(parts))
    depth, out_width = width * sources, flat[0].shape[1]
    strip = min(512, out_width)
    specs = [whole(chunk.shape) for chunk in chunks]
    specs += [pl.BlockSpec((part.shape[0], strip), lambda at, _: (0, at)) for part in flat]
    specs += [pl.BlockSpec(memory_space=pl.ANY)] * (so_far is not None)
    extra = () if so_far is None else (so_far,)
    return pl.pallas_call(
        functools.partial(project_body, count=len(chunks), parts_of=tuple(parts_of)),
        name="project",
        out_shape=jax.ShapeDtypeStruct((tokens, out_width), BF16),
        grid_spec=pltpu.PrefetchScalarGridSpec(
            num_scalar_prefetch=1,
            grid=(out_width // strip,),
            in_specs=specs,
            out_specs=pl.BlockSpec(
                (pl.Element(count), pl.Element(strip)), lambda at, _: (first, at * strip)
            ),
        ),
        input_output_aliases={} if so_far is None else {len(specs): 0},
        compiler_params=pltpu.CompilerParams(vmem_limit_bytes=VMEM),
        cost_estimate=pl.CostEstimate(
            flops=2 * count * depth * out_width,
            bytes_accessed=2 * (count * depth + depth * out_width + count * out_width),
            transcendentals=0,
        ),
    )(place, *chunks, *flat, *extra)


def per_device(
    sizes, query, keys, values, mem_init, beta, mem_gain, loc_gain, w_out
):
    seq_size, head_size = sizes
    tokens, width = query.shape
    dests = head_size * SEG // tokens
    per_dest = SEG // dests // BLOCK
    place = jnp.stack([lax.axis_index("head"), lax.axis_index("seq") % 2]).astype(jnp.int32)
    mem_gain, loc_gain = mem_gain.reshape(1, width), loc_gain.reshape(1, width)

    gather = RowGather(w_out, seq_size, head_size)
    gather.near()
    terms, total = kv_terms(keys, values)
    memory_base = mem_init
    for step in range(1, seq_size):
        memory_base = memory_base + lax.ppermute(
            total, "seq", [(at, at + step) for at in range(seq_size - step)]
        )
    memory_prefix = (memory_base * tokens ** (-0.5))[None]

    if per_dest > 2:
        groups = [(0,), tuple(range(1, per_dest - 1)), (per_dest - 1,)]
    else:
        groups = [(at,) for at in range(per_dest)]
    *near, last = range(2, head_size, 2)
    arrived, after = [], ()
    for blocks in groups:
        run = functools.partial(chunk_call, blocks=blocks, dests=dests, query=query)
        if blocks == groups[0]:
            local = run("local", arrays=[keys, values, beta, loc_gain])
            chunk = run("mix", arrays=[local, memory_base, terms, beta, mem_gain])
            after = gather.now(1, *near)
        else:
            chunk = run(
                "both",
                arrays=[keys, values, memory_base, terms, beta, mem_gain, loc_gain],
                after=tuple(after),
            )
        if blocks == groups[1]:
            for turn in near:
                gather.across(turn)
            after = gather.now(*[turn + 1 for turn in near])
            gather.swap(near[0])
            chunk, early = lax.optimization_barrier((chunk, gather.now(near[0], last)))
            gather.pieces[last] = [early.pop()]
            gather.pieces[near[0]] = early
            for turn in near[1:]:
                gather.swap(turn)
        if blocks == groups[-1]:
            turns = (*near, last)
            _, held = lax.optimization_barrier((chunk, [gather.pieces[turn] for turn in turns]))
            gather.pieces.update(zip(turns, held))
            gather.swap(last)
            for turn in turns:
                gather.across(turn)
        arrived.append(lax.all_to_all(chunk, "head", split_axis=0, concat_axis=0, tiled=True))
    pieces = gather.all()
    rows = tokens // head_size
    last = len(groups[-1]) * BLOCK
    out = project(place, arrived[:-1], pieces, 0, rows)
    out = project(place, arrived[-1:], pieces, rows - last, rows, out)
    return out, memory_prefix


def solution(mesh):
    sizes = (mesh.shape["seq"], mesh.shape["head"])
    in_specs = (
        P("seq", "head"),
        P("seq", "head"),
        P("seq", "head"),
        P("head", None, None),
        P("head"),
        P("head"),
        P("head"),
        P("head", None),
    )
    out_specs = (P(("seq", "head"), None), P("seq", "head", None, None))
    return jax.shard_map(
        functools.partial(per_device, sizes),
        mesh=mesh,
        in_specs=in_specs,
        out_specs=out_specs,
        check_vma=False,
    )
```

```python
import functools

import jax
import jax.numpy as jnp
from jax import lax
from jax.experimental import pallas as pl
from jax.experimental.pallas import tpu as pltpu
from jax.sharding import PartitionSpec as P

HD = 128
SEG = 2048
BLOCK = 256
EPS = 1e-06
LOG2E = 1.4426950408889634
VMEM = 60 << 20
PROJECT_VMEM = 44 << 20
F32, BF16 = jnp.float32, jnp.bfloat16


def call(body, name, out_shape, grid_spec, flops, bytes_accessed, transcendentals=0):
    return pl.pallas_call(
        body,
        name=name,
        out_shape=out_shape,
        grid_spec=grid_spec,
        compiler_params=pltpu.CompilerParams(vmem_limit_bytes=VMEM),
        cost_estimate=pl.CostEstimate(
            flops=flops, bytes_accessed=bytes_accessed, transcendentals=transcendentals
        ),
    )


def whole(shape, memory_space=pltpu.VMEM):
    return pl.BlockSpec(shape, lambda *_: (0,) * len(shape), memory_space=memory_space)


def elu_feature(source):
    wide = source.astype(F32)
    return jnp.where(wide > 0, wide + 1.0, jnp.exp(wide)).astype(BF16)


def columns(head):
    return slice(head * HD, (head + 1) * HD)


def kv_body(k_ref, v_ref, term_ref, total_ref, held):
    for head in range(k_ref.shape[1] // HD):
        cols = columns(head)
        term = lax.dot_general(
            elu_feature(k_ref[:, cols]),
            v_ref[:, cols],
            (((0,), (0,)), ((), ())),
            preferred_element_type=F32,
        )
        term_ref[0, head] = term

        total = jnp.where(pl.program_id(0) == 0, 0.0, held[head]) + term
        held[head] = total
        total_ref[head] = total.astype(BF16)


def kv_terms(keys, values):
    tokens, width = keys.shape
    heads, segs = width // HD, tokens // SEG
    block = pl.BlockSpec((SEG, width), lambda seg: (seg, 0))
    return call(
        kv_body,
        "kv_terms",
        (
            jax.ShapeDtypeStruct((segs, heads, HD, HD), F32),
            jax.ShapeDtypeStruct((heads, HD, HD), BF16),
        ),
        pl.GridSpec(
            grid=(segs,),
            in_specs=[block, block],
            out_specs=[
                pl.BlockSpec((1, heads, HD, HD), lambda seg: (seg, 0, 0, 0)),
                whole((heads, HD, HD)),
            ],
            scratch_shapes=[pltpu.VMEM((heads, HD, HD), F32)],
        ),
        2 * tokens * width * HD,
        2 * keys.size * 2,
    )(keys, values)


def mean_square(source):
    return jnp.mean(source * source, axis=-1, keepdims=True)


def scores_of(q, k):
    rows, end = q.shape[0], k.shape[0]
    wide = q.astype(F32) * (HD**-0.5 * LOG2E)
    high = wide.astype(BF16)
    low = (wide - high.astype(F32)).astype(BF16)
    scores = lax.dot_general(
        jnp.concatenate([high, low], axis=1),
        jnp.concatenate([k, k], axis=1),
        (((1,), (1,)), ((), ())),
        preferred_element_type=F32,
    )
    row = lax.broadcasted_iota(jnp.int32, (rows, rows), 0)
    col = lax.broadcasted_iota(jnp.int32, (rows, rows), 1)
    diagonal = jnp.where(col <= row, scores[:, end - rows :], -jnp.inf)
    if end > rows:
        return jnp.concatenate([scores[:, : end - rows], diagonal], axis=1)
    return diagonal


def local_branch(scores, v, scale_gain):
    largest = jnp.max(scores, axis=-1, keepdims=True)
    weights = jnp.exp2(scores - largest).astype(BF16)
    summed = jnp.dot(
        weights, jnp.concatenate([v, jnp.ones_like(v)], axis=1), preferred_element_type=F32
    )
    local, denominator = summed[:, :HD], summed[:, HD:]
    return local * (
        lax.rsqrt(mean_square(local) + EPS * denominator * denominator) * scale_gain
    )


def score_ahead(units, q_ref, k_ref, use):
    def make(unit):
        dest, rows, end, head = unit
        return scores_of(q_ref[0, dest, rows, columns(head)], k_ref[:end, columns(head)])

    ahead = make(units[0])
    for unit, following in zip(units, [*units[1:], None]):
        scores = ahead
        if following is not None:
            ahead = make(following)
        use(unit, scores)


def memory_branch(q, memory_pair, scale_gain):
    both = jnp.dot(elu_feature(q), memory_pair, preferred_element_type=F32)
    read = both[:, :HD] + both[:, HD:]
    return read * (lax.rsqrt(mean_square(read) + EPS) * scale_gain)


def gate_of(beta_ref, head):
    return 1.0 / (1.0 + jnp.exp(-jnp.full((1, HD), beta_ref[head], F32)))


def units_of(dests, per_dest, block, heads):
    start, size = block
    step = BLOCK if size % BLOCK == 0 else size
    return [
        (dest, slice(at, at + step), dest * per_dest + start + at + step, head)
        for dest in range(dests)
        for at in range(0, size, step)
        for head in range(heads)
    ]


def memory_pairs(init_ref, total_refs, term_ref, memory, prefix_ref, prefix_scale):
    @pl.when(pl.program_id(0) == 0)
    def _():
        for head in range(memory.shape[0]):
            now = init_ref[head]
            for total_ref in total_refs:
                now = now + total_ref[head].astype(F32)
            memory[head] = now
            prefix_ref[0, head] = now * prefix_scale

    pairs = []
    for head in range(memory.shape[0]):
        now = memory[head]
        high = now.astype(BF16)
        low = (now - high.astype(F32)).astype(BF16)
        pairs.append(jnp.concatenate([high, low], axis=1))
        memory[head] = now + term_ref[0, head]
    return pairs


def chunk_body(
    block,
    per_dest,
    prefix_scale,
    earlier,
    q_ref,
    k_ref,
    v_ref,
    init_ref,
    term_ref,
    beta_ref,
    mem_gain_ref,
    loc_gain_ref,
    *rest,
):
    *_, out_ref, prefix_ref, memory = rest
    _, dests, _, width = q_ref.shape
    pairs = memory_pairs(
        init_ref, rest[:earlier], term_ref, memory, prefix_ref, prefix_scale
    )

    def use(unit, scores):
        dest, rows, end, head = unit
        cols = columns(head)
        gate = gate_of(beta_ref, head)
        local = local_branch(scores, v_ref[:end, cols], (1.0 - gate) * loc_gain_ref[:, cols])
        read = memory_branch(q_ref[0, dest, rows, cols], pairs[head], gate * mem_gain_ref[:, cols])
        out_ref[dest, rows, cols] = (read + local).astype(BF16)

    score_ahead(units_of(dests, per_dest, block, width // HD), q_ref, k_ref, use)


def chunk_call(block, dests, arrays, totals, after, cost=1):
    query, keys, values, init, terms, beta, mem_gain, loc_gain = arrays
    tokens, width = query.shape
    segs, heads = tokens // SEG, width // HD
    per_dest = SEG // dests
    start, size = block
    q = query.reshape(segs, dests, per_dest, width)
    q_block = tuple(map(pl.Element, (1, dests, size, width)))
    segment = pl.BlockSpec((SEG, width), lambda seg: (seg, 0))
    prefix_shape = (1, heads, HD, HD)
    pairs_met = segs * heads * size * sum(dest * per_dest + start + size for dest in range(dests))
    return call(
        functools.partial(chunk_body, block, per_dest, tokens**-0.5, len(totals)),
        "attention",
        [
            jax.ShapeDtypeStruct((segs * dests, size, width), BF16),
            jax.ShapeDtypeStruct(prefix_shape, F32),
        ],
        pl.GridSpec(
            grid=(segs,),
            in_specs=[
                pl.BlockSpec(q_block, lambda seg: (seg, 0, start, 0)),
                segment,
                segment,
                whole(init.shape),
                pl.BlockSpec((1, heads, HD, HD), lambda seg: (seg, 0, 0, 0)),
                pl.BlockSpec(memory_space=pltpu.SMEM),
                whole(mem_gain.shape),
                whole(loc_gain.shape),
                *[whole(init.shape)] * len(totals),
                *[pl.BlockSpec(memory_space=pl.ANY)] * len(after),
            ],
            out_specs=[
                pl.BlockSpec((dests, size, width), lambda seg: (seg, 0, 0)),
                whole(prefix_shape),
            ],
            scratch_shapes=[pltpu.VMEM((heads, HD, HD), F32)],
        ),
        int(cost * 8 * pairs_met * HD),
        int(cost * 6 * tokens * width),
        int(cost * pairs_met),
    )(q, *arrays[1:], *totals, *after)


def flip(array, axis, size, turn):
    return lax.ppermute(array, axis, [(at, at ^ turn) for at in range(size)])


class RowGather:
    def __init__(self, w_out, seq_size, head_size):
        half = w_out.shape[0] // 2
        self.seq_size, self.head_size = seq_size, head_size
        self.paired = seq_size % 2 == 0 and half % HD == 0
        own = w_out
        if self.paired:
            own = lax.dynamic_slice_in_dim(w_out, lax.axis_index("seq") % 2 * half, half, 0)
        self.pieces = {0: [w_out]}
        self.own = own

    def near(self):
        for turn in range(2, self.head_size, 2):
            self.pieces[turn] = [flip(self.own, "head", self.head_size, turn)]

    def swap(self, turn):
        if self.paired:
            self.pieces[turn].append(flip(self.pieces[turn][0], "seq", self.seq_size, 1))

    def across(self, turn):
        done = self.pieces.setdefault(turn + 1, [])
        for piece in self.pieces[turn][len(done) :]:
            done.append(flip(piece, "head", self.head_size, 1))

    def now(self, *turns):
        return [piece for turn in turns for piece in self.pieces[turn]]

    def all(self):
        return [tuple(self.pieces[turn]) for turn in range(self.head_size)]


def project_body(place_ref, *refs, parts_of, first, groups):
    row_ref, w_refs = refs[0], refs[1 : 1 + sum(parts_of)]
    out_ref, row_held, total, out_held, w_held, sems = refs[-6:]
    count, out_width = out_held.shape
    width = row_ref.shape[2]
    row_copy = pltpu.make_async_copy(row_ref, row_held, sems.at[len(w_refs)])
    row_copy.start()
    copies, places = [], []
    for turn, parts in enumerate(parts_of):
        source, size = place_ref[0] ^ turn, width // parts
        for part in range(parts):
            at, row = len(copies), turn * width + part * size
            copies.append(pltpu.make_async_copy(w_refs[at], w_held.at[row : row + size], sems.at[at]))
            copies[-1].start()
            place = part if parts == 1 else place_ref[1] ^ part
            places.append((turn, source, pl.ds(pl.multiple_of(place * size, size), size)))
    row_copy.wait()
    step = len(parts_of) // groups
    strip = out_width // groups
    sends = []
    for group in range(groups):
        found = []
        for copy, (turn, source, cols) in zip(copies, places):
            if turn // step == group:
                copy.wait()
                found.append(row_held[source, :, cols])
        rows = jnp.concatenate(found, axis=1)
        met = slice(group * step * width, (group + 1) * step * width)
        for at in range(groups):
            cols = slice(at * strip, (at + 1) * strip)
            term = jnp.dot(rows, w_held[met, cols], preferred_element_type=F32)
            if group > 0:
                term = total[:, cols] + term
            if group < groups - 1:
                total[:, cols] = term
            else:
                out_held[:, cols] = term.astype(BF16)
                sends.append(
                    pltpu.make_async_copy(
                        out_held.at[:, cols],
                        out_ref.at[first : first + count, cols],
                        sems.at[len(w_refs) + 1 + at],
                    )
                )
                sends[-1].start()
    for send in sends:
        send.wait()


def project(place, chunk, pieces, first, tokens, so_far=None):
    sources, count, width = chunk.shape
    flat = [part for piece in pieces for part in piece]
    depth, out_width = width * sources, flat[0].shape[1]
    groups = 4 if sources % 4 == 0 and out_width % 512 == 0 else 1
    extra = () if so_far is None else (so_far,)
    operands = (chunk, *flat, *extra)
    anywhere = pl.BlockSpec(memory_space=pl.ANY)
    return pl.pallas_call(
        functools.partial(
            project_body, parts_of=tuple(map(len, pieces)), first=first, groups=groups
        ),
        name="project",
        out_shape=jax.ShapeDtypeStruct((tokens, out_width), BF16),
        grid_spec=pltpu.PrefetchScalarGridSpec(
            num_scalar_prefetch=1,
            grid=(1,),
            in_specs=[anywhere] * len(operands),
            out_specs=anywhere,
            scratch_shapes=[
                pltpu.VMEM(chunk.shape, BF16),
                pltpu.VMEM((count, out_width), F32),
                pltpu.VMEM((count, out_width), BF16),
                pltpu.VMEM((depth, out_width), BF16),
                pltpu.SemaphoreType.DMA((len(flat) + 1 + groups,)),
            ],
        ),
        input_output_aliases={} if so_far is None else {len(operands): 0},
        compiler_params=pltpu.CompilerParams(vmem_limit_bytes=PROJECT_VMEM),
        cost_estimate=pl.CostEstimate(
            flops=2 * count * depth * out_width,
            bytes_accessed=2 * (count * depth + depth * out_width + count * out_width),
            transcendentals=0,
        ),
    )(place, *operands)


def per_device(
    sizes, query, keys, values, mem_init, beta, mem_gain, loc_gain, w_out
):
    seq_size, head_size = sizes
    tokens, width = query.shape
    dests = head_size * SEG // tokens
    per_dest = SEG // dests
    me, now = lax.axis_index("head"), lax.axis_index("seq")
    place = jnp.stack([me, now % 2]).astype(jnp.int32)
    mem_gain, loc_gain = mem_gain.reshape(1, width), loc_gain.reshape(1, width)

    gather = RowGather(w_out, seq_size, head_size)
    gather.near()
    terms, total = kv_terms(keys, values)
    totals = [
        lax.ppermute(total, "seq", [(at, at + step) for at in range(seq_size - step)])
        for step in range(1, seq_size)
    ]

    groups = [(0, per_dest // 2), (per_dest // 2, per_dest // 2)]
    *near, last = range(2, head_size, 2)
    arrays = (query, keys, values, mem_init, terms, beta, mem_gain, loc_gain)
    arrived, after = [], ()
    for block in groups:
        first = block == groups[0]
        chunk, prefix = chunk_call(block, dests, arrays, totals, after, 0.01 if first else 20)
        if first:
            memory_prefix = prefix
            after = gather.now(*near, last)
        else:
            for turn in near:
                gather.swap(turn)
            chunk, early = lax.optimization_barrier((chunk, [gather.pieces[turn] for turn in near]))
            gather.pieces.update(zip(near, early))
            _, held = lax.optimization_barrier((chunk, gather.pieces[last]))
            gather.pieces[last] = held
            gather.swap(last)
            for turn in (0, *near, last):
                gather.across(turn)
        arrived.append(lax.all_to_all(chunk, "head", split_axis=0, concat_axis=0, tiled=True))
    pieces = gather.all()
    out = None
    for (start, _), chunk in zip(groups, arrived):
        out = project(place, chunk, pieces, start, tokens // head_size, out)
    return out, memory_prefix


def solution(mesh):
    sizes = (mesh.shape["seq"], mesh.shape["head"])
    in_specs = (
        P("seq", "head"),
        P("seq", "head"),
        P("seq", "head"),
        P("head", None, None),
        P("head"),
        P("head"),
        P("head"),
        P("head", None),
    )
    out_specs = (P(("seq", "head"), None), P("seq", "head", None, None))
    return jax.shard_map(
        functools.partial(per_device, sizes),
        mesh=mesh,
        in_specs=in_specs,
        out_specs=out_specs,
        check_vma=False,
    )
```

```python
import functools

import jax
import jax.numpy as jnp
from jax import lax
from jax.experimental import pallas as pl
from jax.experimental.pallas import tpu as pltpu
from jax.sharding import PartitionSpec as P

HD = 128
SEG = 2048
BLOCK = 512
EPS = 1e-06
LOG2E = 1.4426950408889634
VMEM = 60 << 20
PROJECT_VMEM = 30 << 20
F32, BF16 = jnp.float32, jnp.bfloat16


def call(body, name, out_shape, grid_spec, flops, bytes_accessed, transcendentals=0):
    return pl.pallas_call(
        body,
        name=name,
        out_shape=out_shape,
        grid_spec=grid_spec,
        compiler_params=pltpu.CompilerParams(vmem_limit_bytes=VMEM),
        cost_estimate=pl.CostEstimate(
            flops=flops, bytes_accessed=bytes_accessed, transcendentals=transcendentals
        ),
    )


def whole(shape, memory_space=pltpu.VMEM):
    return pl.BlockSpec(shape, lambda *_: (0,) * len(shape), memory_space=memory_space)


def elu_feature(source):
    wide = source.astype(F32)
    return jnp.where(wide > 0, wide + 1.0, jnp.exp(wide)).astype(BF16)


def columns(head):
    return slice(head * HD, (head + 1) * HD)


def kv_body(k_ref, v_ref, term_ref, total_ref, held):
    for head in range(k_ref.shape[1] // HD):
        cols = columns(head)
        term = lax.dot_general(
            elu_feature(k_ref[:, cols]),
            v_ref[:, cols],
            (((0,), (0,)), ((), ())),
            preferred_element_type=F32,
        )
        term_ref[0, head] = term

        total = jnp.where(pl.program_id(0) == 0, 0.0, held[head]) + term
        held[head] = total
        total_ref[head] = total.astype(BF16)


def kv_terms(keys, values):
    tokens, width = keys.shape
    heads, segs = width // HD, tokens // SEG
    block = pl.BlockSpec((SEG, width), lambda seg: (seg, 0))
    return call(
        kv_body,
        "kv_terms",
        (
            jax.ShapeDtypeStruct((segs, heads, HD, HD), F32),
            jax.ShapeDtypeStruct((heads, HD, HD), BF16),
        ),
        pl.GridSpec(
            grid=(segs,),
            in_specs=[block, block],
            out_specs=[
                pl.BlockSpec((1, heads, HD, HD), lambda seg: (seg, 0, 0, 0)),
                whole((heads, HD, HD)),
            ],
            scratch_shapes=[pltpu.VMEM((heads, HD, HD), F32)],
        ),
        2 * tokens * width * HD,
        2 * keys.size * 2,
    )(keys, values)


def mean_square(source):
    return jnp.mean(source * source, axis=-1, keepdims=True)


def scores_of(q, k):
    rows, end = q.shape[0], k.shape[0]
    wide = q.astype(F32) * (HD**-0.5 * LOG2E)
    high = wide.astype(BF16)
    low = (wide - high.astype(F32)).astype(BF16)
    scores = lax.dot_general(
        jnp.concatenate([high, low], axis=1),
        jnp.concatenate([k, k], axis=1),
        (((1,), (1,)), ((), ())),
        preferred_element_type=F32,
    )
    row = lax.broadcasted_iota(jnp.int32, (rows, rows), 0)
    col = lax.broadcasted_iota(jnp.int32, (rows, rows), 1)
    diagonal = jnp.where(col <= row, scores[:, end - rows :], -jnp.inf)
    if end > rows:
        return jnp.concatenate([scores[:, : end - rows], diagonal], axis=1)
    return diagonal


def weights_of(scores):
    largest = jnp.max(scores, axis=-1, keepdims=True)
    return jnp.exp2(scores - largest).astype(BF16)


def local_branch(weights, v, scale_gain):
    summed = jnp.dot(
        weights, jnp.concatenate([v, jnp.ones_like(v)], axis=1), preferred_element_type=F32
    )
    local, denominator = summed[:, :HD], summed[:, HD:]
    return local * (
        lax.rsqrt(mean_square(local) + EPS * denominator * denominator) * scale_gain
    )


def score_ahead(units, q_ref, k_ref, use):
    def make(unit):
        dest, rows, end, head = unit
        return scores_of(q_ref[0, dest, rows, columns(head)], k_ref[:end, columns(head)])

    ahead, behind = make(units[0]), None
    for unit, following in zip(units, [*units[1:], None]):
        scores = ahead
        if following is not None:
            ahead = make(following)
        weights = weights_of(scores)
        if behind is not None:
            use(*behind)
        behind = unit, weights
    use(*behind)


def memory_branch(q, memory_pair, scale_gain):
    both = jnp.dot(elu_feature(q), memory_pair, preferred_element_type=F32)
    read = both[:, :HD] + both[:, HD:]
    return read * (lax.rsqrt(mean_square(read) + EPS) * scale_gain)


def gate_of(beta_ref, head):
    return 1.0 / (1.0 + jnp.exp(-jnp.full((1, HD), beta_ref[head], F32)))


def units_of(dests, per_dest, block, heads):
    start, size = block
    step = BLOCK if size % BLOCK == 0 else size
    return [
        (dest, slice(at, at + step), dest * per_dest + start + at + step, head)
        for dest in range(dests)
        for at in range(0, size, step)
        for head in range(heads)
    ]


def memory_pairs(init_ref, total_refs, term_ref, memory, prefix_ref, prefix_scale):
    @pl.when(pl.program_id(0) == 0)
    def _():
        for head in range(memory.shape[0]):
            now = init_ref[head]
            for total_ref in total_refs:
                now = now + total_ref[head].astype(F32)
            memory[head] = now
            prefix_ref[0, head] = now * prefix_scale

    pairs = []
    for head in range(memory.shape[0]):
        now = memory[head]
        high = now.astype(BF16)
        low = (now - high.astype(F32)).astype(BF16)
        pairs.append(jnp.concatenate([high, low], axis=1))
        memory[head] = now + term_ref[0, head]
    return pairs


def chunk_body(
    block,
    per_dest,
    prefix_scale,
    earlier,
    q_ref,
    k_ref,
    v_ref,
    init_ref,
    term_ref,
    beta_ref,
    mem_gain_ref,
    loc_gain_ref,
    *rest,
):
    *_, out_ref, prefix_ref, memory = rest
    _, dests, _, width = q_ref.shape
    pairs = memory_pairs(
        init_ref, rest[:earlier], term_ref, memory, prefix_ref, prefix_scale
    )

    def use(unit, weights):
        dest, rows, end, head = unit
        cols = columns(head)
        gate = gate_of(beta_ref, head)
        local = local_branch(weights, v_ref[:end, cols], (1.0 - gate) * loc_gain_ref[:, cols])
        read = memory_branch(q_ref[0, dest, rows, cols], pairs[head], gate * mem_gain_ref[:, cols])
        out_ref[dest, rows, cols] = (read + local).astype(BF16)

    score_ahead(units_of(dests, per_dest, block, width // HD), q_ref, k_ref, use)


def chunk_call(block, dests, arrays, totals, after, cost=1):
    query, keys, values, init, terms, beta, mem_gain, loc_gain = arrays
    tokens, width = query.shape
    segs, heads = tokens // SEG, width // HD
    per_dest = SEG // dests
    start, size = block
    q = query.reshape(segs, dests, per_dest, width)
    q_block = tuple(map(pl.Element, (1, dests, size, width)))
    met = (dests - 1) * per_dest + start + size
    segment = pl.BlockSpec((pl.Element(met), pl.Element(width)), lambda seg: (seg * SEG, 0))
    prefix_shape = (1, heads, HD, HD)
    pairs_met = segs * heads * size * sum(dest * per_dest + start + size for dest in range(dests))
    return call(
        functools.partial(chunk_body, block, per_dest, tokens**-0.5, len(totals)),
        "attention",
        [
            jax.ShapeDtypeStruct((segs * dests, size, width), BF16),
            jax.ShapeDtypeStruct(prefix_shape, F32),
        ],
        pl.GridSpec(
            grid=(segs,),
            in_specs=[
                pl.BlockSpec(q_block, lambda seg: (seg, 0, start, 0)),
                segment,
                segment,
                whole(init.shape),
                pl.BlockSpec((1, heads, HD, HD), lambda seg: (seg, 0, 0, 0)),
                pl.BlockSpec(memory_space=pltpu.SMEM),
                whole(mem_gain.shape),
                whole(loc_gain.shape),
                *[whole(init.shape)] * len(totals),
                *[pl.BlockSpec(memory_space=pl.ANY)] * len(after),
            ],
            out_specs=[
                pl.BlockSpec((dests, size, width), lambda seg: (seg, 0, 0)),
                whole(prefix_shape),
            ],
            scratch_shapes=[pltpu.VMEM((heads, HD, HD), F32)],
        ),
        int(cost * 8 * pairs_met * HD),
        int(cost * 6 * tokens * width),
        int(cost * pairs_met),
    )(q, *arrays[1:], *totals, *after)


def flip(array, axis, size, turn):
    return lax.ppermute(array, axis, [(at, at ^ turn) for at in range(size)])


class RowGather:
    def __init__(self, w_out, seq_size, head_size):
        half = w_out.shape[0] // 2
        self.seq_size, self.head_size = seq_size, head_size
        self.paired = seq_size % 2 == 0 and half % HD == 0
        own = w_out
        if self.paired:
            own = lax.dynamic_slice_in_dim(w_out, lax.axis_index("seq") % 2 * half, half, 0)
        self.pieces = {0: [w_out]}
        self.own = own

    def near(self):
        for turn in range(2, self.head_size, 2):
            self.pieces[turn] = [flip(self.own, "head", self.head_size, turn)]

    def swap(self, turn):
        if self.paired:
            self.pieces[turn].append(flip(self.pieces[turn][0], "seq", self.seq_size, 1))

    def across(self, turn):
        done = self.pieces.setdefault(turn + 1, [])
        for piece in self.pieces[turn][len(done) :]:
            done.append(flip(piece, "head", self.head_size, 1))

    def now(self, *turns):
        return [piece for turn in turns for piece in self.pieces[turn]]

    def all(self):
        return [tuple(self.pieces[turn]) for turn in range(self.head_size)]


def project_body(place_ref, *refs, parts_of, first, groups):
    row_ref, w_refs = refs[0], refs[1 : 1 + sum(parts_of)]
    out_ref, row_held, total, out_held, w_held, sems = refs[-6:]
    count, out_width = out_held.shape
    width = row_ref.shape[2]
    row_copy = pltpu.make_async_copy(row_ref, row_held, sems.at[len(w_refs)])
    row_copy.start()
    copies, places = [], []
    for turn, parts in enumerate(parts_of):
        source, size = place_ref[0] ^ turn, width // parts
        for part in range(parts):
            at, row = len(copies), turn * width + part * size
            copies.append(pltpu.make_async_copy(w_refs[at], w_held.at[row : row + size], sems.at[at]))
            place = part if parts == 1 else place_ref[1] ^ part
            places.append((turn, source, pl.ds(pl.multiple_of(place * size, size), size)))
    step = len(parts_of) // groups
    strip = out_width // groups

    def fetch(group):
        for copy, (turn, _, _) in zip(copies, places):
            if turn // step == group:
                copy.start()

    ahead = 2
    for group in range(min(ahead, groups)):
        fetch(group)
    row_copy.wait()
    sends = []
    for group in range(groups):
        found = []
        for copy, (turn, source, cols) in zip(copies, places):
            if turn // step == group:
                copy.wait()
                found.append(row_held[source, :, cols])
        if group + ahead < groups:
            fetch(group + ahead)
        rows = jnp.concatenate(found, axis=1)
        met = slice(group * step * width, (group + 1) * step * width)
        for at in range(groups):
            cols = slice(at * strip, (at + 1) * strip)
            term = jnp.dot(rows, w_held[met, cols], preferred_element_type=F32)
            if group > 0:
                term = total[:, cols] + term
            if group < groups - 1:
                total[:, cols] = term
            else:
                out_held[:, cols] = term.astype(BF16)
                sends.append(
                    pltpu.make_async_copy(
                        out_held.at[:, cols],
                        out_ref.at[first : first + count, cols],
                        sems.at[len(w_refs) + 1 + at],
                    )
                )
                sends[-1].start()
    for send in sends:
        send.wait()


def project(place, chunk, pieces, first, tokens, so_far=None):
    sources, count, width = chunk.shape
    flat = [part for piece in pieces for part in piece]
    depth, out_width = width * sources, flat[0].shape[1]
    groups = 4 if sources % 4 == 0 and out_width % 512 == 0 else 1
    extra = () if so_far is None else (so_far,)
    operands = (chunk, *flat, *extra)
    anywhere = pl.BlockSpec(memory_space=pl.ANY)
    return pl.pallas_call(
        functools.partial(
            project_body, parts_of=tuple(map(len, pieces)), first=first, groups=groups
        ),
        name="project",
        out_shape=jax.ShapeDtypeStruct((tokens, out_width), BF16),
        grid_spec=pltpu.PrefetchScalarGridSpec(
            num_scalar_prefetch=1,
            grid=(1,),
            in_specs=[anywhere] * len(operands),
            out_specs=anywhere,
            scratch_shapes=[
                pltpu.VMEM(chunk.shape, BF16),
                pltpu.VMEM((count, out_width), F32),
                pltpu.VMEM((count, out_width), BF16),
                pltpu.VMEM((depth, out_width), BF16),
                pltpu.SemaphoreType.DMA((len(flat) + 1 + groups,)),
            ],
        ),
        input_output_aliases={} if so_far is None else {len(operands): 0},
        compiler_params=pltpu.CompilerParams(vmem_limit_bytes=PROJECT_VMEM),
        cost_estimate=pl.CostEstimate(
            flops=2 * count * depth * out_width,
            bytes_accessed=2 * (count * depth + depth * out_width + count * out_width),
            transcendentals=0,
        ),
    )(place, *operands)


def per_device(
    sizes, query, keys, values, mem_init, beta, mem_gain, loc_gain, w_out
):
    seq_size, head_size = sizes
    tokens, width = query.shape
    dests = head_size * SEG // tokens
    per_dest = SEG // dests
    me, now = lax.axis_index("head"), lax.axis_index("seq")
    place = jnp.stack([me, now % 2]).astype(jnp.int32)
    mem_gain, loc_gain = mem_gain.reshape(1, width), loc_gain.reshape(1, width)

    gather = RowGather(w_out, seq_size, head_size)
    gather.near()
    terms, total = kv_terms(keys, values)
    totals = [
        lax.ppermute(total, "seq", [(at, at + step) for at in range(seq_size - step)])
        for step in range(1, seq_size)
    ]

    groups = [(0, per_dest // 2), (per_dest // 2, per_dest // 2)]
    *near, last = range(2, head_size, 2)
    arrays = (query, keys, values, mem_init, terms, beta, mem_gain, loc_gain)
    arrived, after = [], ()
    for block in groups:
        first = block == groups[0]
        chunk, prefix = chunk_call(block, dests, arrays, totals, after, 0.01 if first else 20)
        if first:
            memory_prefix = prefix
            after = gather.now(*near, last)
        else:
            for turn in near:
                gather.swap(turn)
            chunk, early = lax.optimization_barrier((chunk, [gather.pieces[turn] for turn in near]))
            gather.pieces.update(zip(near, early))
            _, held = lax.optimization_barrier((chunk, gather.pieces[last]))
            gather.pieces[last] = held
            gather.swap(last)
            for turn in (0, *near, last):
                gather.across(turn)
        arrived.append(lax.all_to_all(chunk, "head", split_axis=0, concat_axis=0, tiled=True))
    pieces = gather.all()
    out = None
    for (start, _), chunk in zip(groups, arrived):
        out = project(place, chunk, pieces, start, tokens // head_size, out)
    return out, memory_prefix


def solution(mesh):
    sizes = (mesh.shape["seq"], mesh.shape["head"])
    in_specs = (
        P("seq", "head"),
        P("seq", "head"),
        P("seq", "head"),
        P("head", None, None),
        P("head"),
        P("head"),
        P("head"),
        P("head", None),
    )
    out_specs = (P(("seq", "head"), None), P("seq", "head", None, None))
    return jax.shard_map(
        functools.partial(per_device, sizes),
        mesh=mesh,
        in_specs=in_specs,
        out_specs=out_specs,
        check_vma=False,
    )
```

```python
import functools

import jax
import jax.numpy as jnp
from jax import lax
from jax.experimental import pallas as pl
from jax.experimental.pallas import tpu as pltpu
from jax.sharding import PartitionSpec as P

HD = 128
SEG = 2048
BLOCK = 512
EPS = 1e-06
LOG2E = 1.4426950408889634
VMEM = 51 << 20
PROJECT_VMEM = 30 << 20
F32, BF16 = jnp.float32, jnp.bfloat16


def call(body, name, out_shape, grid_spec, flops, bytes_accessed, transcendentals=0):
    return pl.pallas_call(
        body,
        name=name,
        out_shape=out_shape,
        grid_spec=grid_spec,
        compiler_params=pltpu.CompilerParams(vmem_limit_bytes=VMEM),
        cost_estimate=pl.CostEstimate(
            flops=flops, bytes_accessed=bytes_accessed, transcendentals=transcendentals
        ),
    )


def whole(shape, memory_space=pltpu.VMEM):
    return pl.BlockSpec(shape, lambda *_: (0,) * len(shape), memory_space=memory_space)


def elu_feature(source):
    wide = source.astype(F32)
    return jnp.where(wide > 0, wide + 1.0, jnp.exp(wide)).astype(BF16)


def columns(head):
    return slice(head * HD, (head + 1) * HD)


def kv_body(k_ref, v_ref, term_ref, total_ref, held):
    for head in range(k_ref.shape[1] // HD):
        cols = columns(head)
        term = lax.dot_general(
            elu_feature(k_ref[:, cols]),
            v_ref[:, cols],
            (((0,), (0,)), ((), ())),
            preferred_element_type=F32,
        )
        term_ref[0, head] = term

        total = jnp.where(pl.program_id(0) == 0, 0.0, held[head]) + term
        held[head] = total
        total_ref[head] = total.astype(BF16)


def kv_terms(keys, values):
    tokens, width = keys.shape
    heads, segs = width // HD, tokens // SEG
    block = pl.BlockSpec((SEG, width), lambda seg: (seg, 0))
    return call(
        kv_body,
        "kv_terms",
        (
            jax.ShapeDtypeStruct((segs, heads, HD, HD), F32),
            jax.ShapeDtypeStruct((heads, HD, HD), BF16),
        ),
        pl.GridSpec(
            grid=(segs,),
            in_specs=[block, block],
            out_specs=[
                pl.BlockSpec((1, heads, HD, HD), lambda seg: (seg, 0, 0, 0)),
                whole((heads, HD, HD)),
            ],
            scratch_shapes=[pltpu.VMEM((heads, HD, HD), F32)],
        ),
        2 * tokens * width * HD,
        2 * keys.size * 2,
    )(keys, values)


def mean_square(source):
    return jnp.mean(source * source, axis=-1, keepdims=True)


def scores_of(q, k):
    rows, end = q.shape[0], k.shape[0]
    wide = q.astype(F32) * (HD**-0.5 * LOG2E)
    high = wide.astype(BF16)
    low = (wide - high.astype(F32)).astype(BF16)
    scores = lax.dot_general(
        jnp.concatenate([high, low], axis=1),
        jnp.concatenate([k, k], axis=1),
        (((1,), (1,)), ((), ())),
        preferred_element_type=F32,
    )
    row = lax.broadcasted_iota(jnp.int32, (rows, rows), 0)
    col = lax.broadcasted_iota(jnp.int32, (rows, rows), 1)
    diagonal = jnp.where(col <= row, scores[:, end - rows :], -jnp.inf)
    if end > rows:
        return jnp.concatenate([scores[:, : end - rows], diagonal], axis=1)
    return diagonal


def weights_of(scores):
    largest = jnp.max(scores, axis=-1, keepdims=True)
    return jnp.exp2(scores - largest).astype(BF16)


def local_branch(weights, v, scale_gain):
    summed = jnp.dot(
        weights, jnp.concatenate([v, jnp.ones_like(v)], axis=1), preferred_element_type=F32
    )
    local, denominator = summed[:, :HD], summed[:, HD:]
    return local * (
        lax.rsqrt(mean_square(local) + EPS * denominator * denominator) * scale_gain
    )


def score_ahead(units, q_ref, k_ref, use):
    def make(unit):
        dest, rows, end, head = unit
        return scores_of(q_ref[0, dest, rows, columns(head)], k_ref[:end, columns(head)])

    ahead, behind = make(units[0]), None
    for unit, following in zip(units, [*units[1:], None]):
        scores = ahead
        if following is not None:
            ahead = make(following)
        weights = weights_of(scores)
        if behind is not None:
            use(*behind)
        behind = unit, weights
    use(*behind)


def memory_branch(q, memory_pair, scale_gain):
    both = jnp.dot(elu_feature(q), memory_pair, preferred_element_type=F32)
    read = both[:, :HD] + both[:, HD:]
    return read * (lax.rsqrt(mean_square(read) + EPS) * scale_gain)


def gate_of(beta_ref, head):
    return 1.0 / (1.0 + jnp.exp(-jnp.full((1, HD), beta_ref[head], F32)))


def units_of(dests, per_dest, block, heads):
    start, size = block
    step = BLOCK if size % BLOCK == 0 else size
    return [
        (dest, slice(at, at + step), dest * per_dest + start + at + step, head)
        for dest in range(dests)
        for at in range(0, size, step)
        for head in range(heads)
    ]


def memory_pairs(init_ref, total_refs, term_ref, memory, prefix_ref, prefix_scale):
    @pl.when(pl.program_id(0) == 0)
    def _():
        for head in range(memory.shape[0]):
            now = init_ref[head]
            for total_ref in total_refs:
                now = now + total_ref[head].astype(F32)
            memory[head] = now
            prefix_ref[0, head] = now * prefix_scale

    pairs = []
    for head in range(memory.shape[0]):
        now = memory[head]
        high = now.astype(BF16)
        low = (now - high.astype(F32)).astype(BF16)
        pairs.append(jnp.concatenate([high, low], axis=1))
        memory[head] = now + term_ref[0, head]
    return pairs


def chunk_body(
    block,
    per_dest,
    prefix_scale,
    earlier,
    q_ref,
    k_ref,
    v_ref,
    init_ref,
    term_ref,
    beta_ref,
    mem_gain_ref,
    loc_gain_ref,
    *rest,
):
    *_, out_ref, prefix_ref, memory = rest
    _, dests, _, width = q_ref.shape
    pairs = memory_pairs(
        init_ref, rest[:earlier], term_ref, memory, prefix_ref, prefix_scale
    )

    def use(unit, weights):
        dest, rows, end, head = unit
        cols = columns(head)
        gate = gate_of(beta_ref, head)
        local = local_branch(weights, v_ref[:end, cols], (1.0 - gate) * loc_gain_ref[:, cols])
        read = memory_branch(q_ref[0, dest, rows, cols], pairs[head], gate * mem_gain_ref[:, cols])
        out_ref[dest, rows, cols] = (read + local).astype(BF16)

    score_ahead(units_of(dests, per_dest, block, width // HD), q_ref, k_ref, use)


def chunk_call(block, dests, arrays, totals, after, cost=1):
    query, keys, values, init, terms, beta, mem_gain, loc_gain = arrays
    tokens, width = query.shape
    segs, heads = tokens // SEG, width // HD
    per_dest = SEG // dests
    start, size = block
    q = query.reshape(segs, dests, per_dest, width)
    q_block = tuple(map(pl.Element, (1, dests, size, width)))
    met = (dests - 1) * per_dest + start + size
    segment = pl.BlockSpec((pl.Element(met), pl.Element(width)), lambda seg: (seg * SEG, 0))
    prefix_shape = (1, heads, HD, HD)
    pairs_met = segs * heads * size * sum(dest * per_dest + start + size for dest in range(dests))
    return call(
        functools.partial(chunk_body, block, per_dest, tokens**-0.5, len(totals)),
        "attention",
        [
            jax.ShapeDtypeStruct((segs * dests, size, width), BF16),
            jax.ShapeDtypeStruct(prefix_shape, F32),
        ],
        pl.GridSpec(
            grid=(segs,),
            in_specs=[
                pl.BlockSpec(q_block, lambda seg: (seg, 0, start, 0)),
                segment,
                segment,
                whole(init.shape),
                pl.BlockSpec((1, heads, HD, HD), lambda seg: (seg, 0, 0, 0)),
                pl.BlockSpec(memory_space=pltpu.SMEM),
                whole(mem_gain.shape),
                whole(loc_gain.shape),
                *[whole(init.shape)] * len(totals),
                *[pl.BlockSpec(memory_space=pl.ANY)] * len(after),
            ],
            out_specs=[
                pl.BlockSpec((dests, size, width), lambda seg: (seg, 0, 0)),
                whole(prefix_shape),
            ],
            scratch_shapes=[pltpu.VMEM((heads, HD, HD), F32)],
        ),
        int(cost * 8 * pairs_met * HD),
        int(cost * 6 * tokens * width),
        int(cost * pairs_met),
    )(q, *arrays[1:], *totals, *after)


def flip(array, axis, size, turn):
    return lax.ppermute(array, axis, [(at, at ^ turn) for at in range(size)])


class RowGather:
    def __init__(self, w_out, seq_size, head_size):
        half = w_out.shape[0] // 2
        self.seq_size, self.head_size = seq_size, head_size
        self.paired = seq_size % 2 == 0 and half % HD == 0
        own = w_out
        if self.paired:
            own = lax.dynamic_slice_in_dim(w_out, lax.axis_index("seq") % 2 * half, half, 0)
        self.pieces = {0: [w_out]}
        self.own = own

    def near(self):
        for turn in range(2, self.head_size, 2):
            self.pieces[turn] = [flip(self.own, "head", self.head_size, turn)]

    def swap(self, turn):
        if self.paired:
            self.pieces[turn].append(flip(self.pieces[turn][0], "seq", self.seq_size, 1))

    def across(self, turn):
        done = self.pieces.setdefault(turn + 1, [])
        for piece in self.pieces[turn][len(done) :]:
            done.append(flip(piece, "head", self.head_size, 1))

    def now(self, *turns):
        return [piece for turn in turns for piece in self.pieces[turn]]

    def all(self):
        return [tuple(self.pieces[turn]) for turn in range(self.head_size)]


def project_body(place_ref, *refs, parts_of, first, groups):
    row_ref, w_refs = refs[0], refs[1 : 1 + sum(parts_of)]
    out_ref, row_held, total, out_held, w_held, sems = refs[-6:]
    count, out_width = out_held.shape
    width = row_ref.shape[2]
    row_copy = pltpu.make_async_copy(row_ref, row_held, sems.at[len(w_refs)])
    row_copy.start()
    copies, places = [], []
    for turn, parts in enumerate(parts_of):
        source, size = place_ref[0] ^ turn, width // parts
        for part in range(parts):
            at, row = len(copies), turn * width + part * size
            copies.append(pltpu.make_async_copy(w_refs[at], w_held.at[row : row + size], sems.at[at]))
            place = part if parts == 1 else place_ref[1] ^ part
            places.append((turn, source, pl.ds(pl.multiple_of(place * size, size), size)))
    step = len(parts_of) // groups
    strip = out_width // groups

    def fetch(group):
        for copy, (turn, _, _) in zip(copies, places):
            if turn // step == group:
                copy.start()

    ahead = 2
    for group in range(min(ahead, groups)):
        fetch(group)
    row_copy.wait()
    sends = []
    for group in range(groups):
        found = []
        for copy, (turn, source, cols) in zip(copies, places):
            if turn // step == group:
                copy.wait()
                found.append(row_held[source, :, cols])
        if group + ahead < groups:
            fetch(group + ahead)
        rows = jnp.concatenate(found, axis=1)
        met = slice(group * step * width, (group + 1) * step * width)
        for at in range(groups):
            cols = slice(at * strip, (at + 1) * strip)
            term = jnp.dot(rows, w_held[met, cols], preferred_element_type=F32)
            if group > 0:
                term = total[:, cols] + term
            if group < groups - 1:
                total[:, cols] = term
            else:
                out_held[:, cols] = term.astype(BF16)
                sends.append(
                    pltpu.make_async_copy(
                        out_held.at[:, cols],
                        out_ref.at[first : first + count, cols],
                        sems.at[len(w_refs) + 1 + at],
                    )
                )
                sends[-1].start()
    for send in sends:
        send.wait()


def project(place, chunk, pieces, first, tokens, so_far=None):
    sources, count, width = chunk.shape
    flat = [part for piece in pieces for part in piece]
    depth, out_width = width * sources, flat[0].shape[1]
    groups = 4 if sources % 4 == 0 and out_width % 512 == 0 else 1
    extra = () if so_far is None else (so_far,)
    operands = (chunk, *flat, *extra)
    anywhere = pl.BlockSpec(memory_space=pl.ANY)
    return pl.pallas_call(
        functools.partial(
            project_body, parts_of=tuple(map(len, pieces)), first=first, groups=groups
        ),
        name="project",
        out_shape=jax.ShapeDtypeStruct((tokens, out_width), BF16),
        grid_spec=pltpu.PrefetchScalarGridSpec(
            num_scalar_prefetch=1,
            grid=(1,),
            in_specs=[anywhere] * len(operands),
            out_specs=anywhere,
            scratch_shapes=[
                pltpu.VMEM(chunk.shape, BF16),
                pltpu.VMEM((count, out_width), F32),
                pltpu.VMEM((count, out_width), BF16),
                pltpu.VMEM((depth, out_width), BF16),
                pltpu.SemaphoreType.DMA((len(flat) + 1 + groups,)),
            ],
        ),
        input_output_aliases={} if so_far is None else {len(operands): 0},
        compiler_params=pltpu.CompilerParams(vmem_limit_bytes=PROJECT_VMEM),
        cost_estimate=pl.CostEstimate(
            flops=2 * count * depth * out_width,
            bytes_accessed=2 * (count * depth + depth * out_width + count * out_width),
            transcendentals=0,
        ),
    )(place, *operands)


def per_device(
    sizes, query, keys, values, mem_init, beta, mem_gain, loc_gain, w_out
):
    seq_size, head_size = sizes
    tokens, width = query.shape
    dests = head_size * SEG // tokens
    per_dest = SEG // dests
    me, now = lax.axis_index("head"), lax.axis_index("seq")
    place = jnp.stack([me, now % 2]).astype(jnp.int32)
    mem_gain, loc_gain = mem_gain.reshape(1, width), loc_gain.reshape(1, width)

    gather = RowGather(w_out, seq_size, head_size)
    gather.near()
    terms, total = kv_terms(keys, values)
    totals = [
        lax.ppermute(total, "seq", [(at, at + step) for at in range(seq_size - step)])
        for step in range(1, seq_size)
    ]

    groups = [(0, per_dest // 2), (per_dest // 2, per_dest // 2)]
    *near, last = range(2, head_size, 2)
    arrays = (query, keys, values, mem_init, terms, beta, mem_gain, loc_gain)
    arrived, after = [], ()
    for block in groups:
        first = block == groups[0]
        chunk, prefix = chunk_call(block, dests, arrays, totals, after, 0.01 if first else 20)
        if first:
            memory_prefix = prefix
            after = gather.now(*near, last)
        else:
            for turn in near:
                gather.swap(turn)
            chunk, early = lax.optimization_barrier((chunk, [gather.pieces[turn] for turn in near]))
            gather.pieces.update(zip(near, early))
            _, held = lax.optimization_barrier((chunk, gather.pieces[last]))
            gather.pieces[last] = held
            gather.swap(last)
            for turn in (0, *near, last):
                gather.across(turn)
        arrived.append(lax.all_to_all(chunk, "head", split_axis=0, concat_axis=0, tiled=True))
    pieces = gather.all()
    out = None
    for (start, _), chunk in zip(groups, arrived):
        out = project(place, chunk, pieces, start, tokens // head_size, out)
    return out, memory_prefix


def solution(mesh):
    sizes = (mesh.shape["seq"], mesh.shape["head"])
    in_specs = (
        P("seq", "head"),
        P("seq", "head"),
        P("seq", "head"),
        P("head", None, None),
        P("head"),
        P("head"),
        P("head"),
        P("head", None),
    )
    out_specs = (P(("seq", "head"), None), P("seq", "head", None, None))
    return jax.shard_map(
        functools.partial(per_device, sizes),
        mesh=mesh,
        in_specs=in_specs,
        out_specs=out_specs,
        check_vma=False,
    )
```

```python
import functools

import jax
import jax.numpy as jnp
from jax import lax
from jax.experimental import pallas as pl
from jax.experimental.pallas import tpu as pltpu
from jax.sharding import PartitionSpec as P

HD = 128
SEG = 2048
BLOCK = 512
EPS = 1e-06
LOG2E = 1.4426950408889634
VMEM = 51 << 20
PROJECT_VMEM = 30 << 20
F32, BF16 = jnp.float32, jnp.bfloat16


def call(body, name, out_shape, grid_spec, flops, bytes_accessed, transcendentals=0):
    return pl.pallas_call(
        body,
        name=name,
        out_shape=out_shape,
        grid_spec=grid_spec,
        compiler_params=pltpu.CompilerParams(vmem_limit_bytes=VMEM),
        cost_estimate=pl.CostEstimate(
            flops=flops, bytes_accessed=bytes_accessed, transcendentals=transcendentals
        ),
    )


def whole(shape, memory_space=pltpu.VMEM):
    return pl.BlockSpec(shape, lambda *_: (0,) * len(shape), memory_space=memory_space)


def elu_feature(source):
    wide = source.astype(F32)
    return jnp.where(wide > 0, wide + 1.0, jnp.exp(wide)).astype(BF16)


def columns(head):
    return slice(head * HD, (head + 1) * HD)


def kv_body(k_ref, v_ref, term_ref, total_ref, held):
    for head in range(k_ref.shape[1] // HD):
        cols = columns(head)
        term = lax.dot_general(
            elu_feature(k_ref[:, cols]),
            v_ref[:, cols],
            (((0,), (0,)), ((), ())),
            preferred_element_type=F32,
        )
        term_ref[0, head] = term

        total = jnp.where(pl.program_id(0) == 0, 0.0, held[head]) + term
        held[head] = total
        total_ref[head] = total.astype(BF16)


def kv_terms(keys, values):
    tokens, width = keys.shape
    heads, segs = width // HD, tokens // SEG
    block = pl.BlockSpec((SEG, width), lambda seg: (seg, 0))
    return call(
        kv_body,
        "kv_terms",
        (
            jax.ShapeDtypeStruct((segs, heads, HD, HD), F32),
            jax.ShapeDtypeStruct((heads, HD, HD), BF16),
        ),
        pl.GridSpec(
            grid=(segs,),
            in_specs=[block, block],
            out_specs=[
                pl.BlockSpec((1, heads, HD, HD), lambda seg: (seg, 0, 0, 0)),
                whole((heads, HD, HD)),
            ],
            scratch_shapes=[pltpu.VMEM((heads, HD, HD), F32)],
        ),
        2 * tokens * width * HD,
        2 * keys.size * 2,
    )(keys, values)


def mean_square(source):
    return jnp.mean(source * source, axis=-1, keepdims=True)


def scores_of(q, k):
    rows, end = q.shape[0], k.shape[0]
    wide = q.astype(F32) * (HD**-0.5 * LOG2E)
    high = wide.astype(BF16)
    low = (wide - high.astype(F32)).astype(BF16)
    scores = lax.dot_general(
        jnp.concatenate([high, low], axis=1),
        jnp.concatenate([k, k], axis=1),
        (((1,), (1,)), ((), ())),
        preferred_element_type=F32,
    )
    row = lax.broadcasted_iota(jnp.int32, (rows, rows), 0)
    col = lax.broadcasted_iota(jnp.int32, (rows, rows), 1)
    diagonal = jnp.where(col <= row, scores[:, end - rows :], -jnp.inf)
    if end > rows:
        return jnp.concatenate([scores[:, : end - rows], diagonal], axis=1)
    return diagonal


def weights_of(scores):
    largest = jnp.max(scores, axis=-1, keepdims=True)
    return jnp.exp2(scores - largest).astype(BF16)


def local_branch(weights, v, scale_gain):
    summed = jnp.dot(
        weights, jnp.concatenate([v, jnp.ones_like(v)], axis=1), preferred_element_type=F32
    )
    local, denominator = summed[:, :HD], summed[:, HD:]
    return local * (
        lax.rsqrt(mean_square(local) + EPS * denominator * denominator) * scale_gain
    )


def score_ahead(units, q_ref, k_ref, use):
    def make(unit):
        dest, rows, end, head = unit
        return scores_of(q_ref[0, dest, rows, columns(head)], k_ref[:end, columns(head)])

    ahead, behind = make(units[0]), None
    for unit, following in zip(units, [*units[1:], None]):
        scores = ahead
        if following is not None:
            ahead = make(following)
        weights = weights_of(scores)
        if behind is not None:
            use(*behind)
        behind = unit, weights
    use(*behind)


def memory_branch(q, memory_pair, scale_gain):
    both = jnp.dot(elu_feature(q), memory_pair, preferred_element_type=F32)
    read = both[:, :HD] + both[:, HD:]
    return read * (lax.rsqrt(mean_square(read) + EPS) * scale_gain)


def gate_of(beta_ref, head):
    return 1.0 / (1.0 + jnp.exp(-jnp.full((1, HD), beta_ref[head], F32)))


def units_of(dests, per_dest, block, heads):
    start, size = block
    step = BLOCK if size % BLOCK == 0 else size
    return [
        (dest, slice(at, at + step), dest * per_dest + start + at + step, head)
        for dest in range(dests)
        for at in range(0, size, step)
        for head in range(heads)
    ]


def memory_pairs(init_ref, total_refs, term_ref, memory, prefix_ref, prefix_scale):
    @pl.when(pl.program_id(0) == 0)
    def _():
        for head in range(memory.shape[0]):
            now = init_ref[head]
            for total_ref in total_refs:
                now = now + total_ref[head].astype(F32)
            memory[head] = now
            prefix_ref[0, head] = now * prefix_scale

    pairs = []
    for head in range(memory.shape[0]):
        now = memory[head]
        high = now.astype(BF16)
        low = (now - high.astype(F32)).astype(BF16)
        pairs.append(jnp.concatenate([high, low], axis=1))
        memory[head] = now + term_ref[0, head]
    return pairs


def chunk_body(
    block,
    per_dest,
    prefix_scale,
    earlier,
    q_ref,
    k_ref,
    v_ref,
    init_ref,
    term_ref,
    beta_ref,
    mem_gain_ref,
    loc_gain_ref,
    *rest,
):
    *_, out_ref, prefix_ref, memory = rest
    _, dests, _, width = q_ref.shape
    pairs = memory_pairs(
        init_ref, rest[:earlier], term_ref, memory, prefix_ref, prefix_scale
    )

    def use(unit, weights):
        dest, rows, end, head = unit
        cols = columns(head)
        gate = gate_of(beta_ref, head)
        local = local_branch(weights, v_ref[:end, cols], (1.0 - gate) * loc_gain_ref[:, cols])
        read = memory_branch(q_ref[0, dest, rows, cols], pairs[head], gate * mem_gain_ref[:, cols])
        out_ref[dest, rows, cols] = (read + local).astype(BF16)

    score_ahead(units_of(dests, per_dest, block, width // HD), q_ref, k_ref, use)


def chunk_call(block, dests, arrays, totals, after, cost=1):
    query, keys, values, init, terms, beta, mem_gain, loc_gain = arrays
    tokens, width = query.shape
    segs, heads = tokens // SEG, width // HD
    per_dest = SEG // dests
    start, size = block
    q = query.reshape(segs, dests, per_dest, width)
    q_block = tuple(map(pl.Element, (1, dests, size, width)))
    met = (dests - 1) * per_dest + start + size
    segment = pl.BlockSpec((pl.Element(met), pl.Element(width)), lambda seg: (seg * SEG, 0))
    prefix_shape = (1, heads, HD, HD)
    pairs_met = segs * heads * size * sum(dest * per_dest + start + size for dest in range(dests))
    return call(
        functools.partial(chunk_body, block, per_dest, tokens**-0.5, len(totals)),
        "attention",
        [
            jax.ShapeDtypeStruct((segs * dests, size, width), BF16),
            jax.ShapeDtypeStruct(prefix_shape, F32),
        ],
        pl.GridSpec(
            grid=(segs,),
            in_specs=[
                pl.BlockSpec(q_block, lambda seg: (seg, 0, start, 0)),
                segment,
                segment,
                whole(init.shape),
                pl.BlockSpec((1, heads, HD, HD), lambda seg: (seg, 0, 0, 0)),
                pl.BlockSpec(memory_space=pltpu.SMEM),
                whole(mem_gain.shape),
                whole(loc_gain.shape),
                *[whole(init.shape)] * len(totals),
                *[pl.BlockSpec(memory_space=pl.ANY)] * len(after),
            ],
            out_specs=[
                pl.BlockSpec((dests, size, width), lambda seg: (seg, 0, 0)),
                whole(prefix_shape),
            ],
            scratch_shapes=[pltpu.VMEM((heads, HD, HD), F32)],
        ),
        int(cost * 8 * pairs_met * HD),
        int(cost * 6 * tokens * width),
        int(cost * pairs_met),
    )(q, *arrays[1:], *totals, *after)


def flip(array, axis, size, turn):
    return lax.ppermute(array, axis, [(at, at ^ turn) for at in range(size)])


class RowGather:
    def __init__(self, w_out, seq_size, head_size):
        half = w_out.shape[0] // 2
        self.seq_size, self.head_size = seq_size, head_size
        self.paired = seq_size % 2 == 0 and half % HD == 0
        own = w_out
        if self.paired:
            own = lax.dynamic_slice_in_dim(w_out, lax.axis_index("seq") % 2 * half, half, 0)
        self.pieces = {0: [w_out]}
        self.own = own

    def near(self):
        for turn in range(2, self.head_size, 2):
            self.pieces[turn] = [flip(self.own, "head", self.head_size, turn)]

    def swap(self, turn):
        if self.paired:
            self.pieces[turn].append(flip(self.pieces[turn][0], "seq", self.seq_size, 1))

    def across(self, turn):
        done = self.pieces.setdefault(turn + 1, [])
        for piece in self.pieces[turn][len(done) :]:
            done.append(flip(piece, "head", self.head_size, 1))

    def now(self, *turns):
        return [piece for turn in turns for piece in self.pieces[turn]]

    def all(self):
        return [tuple(self.pieces[turn]) for turn in range(self.head_size)]


def project_body(place_ref, *refs, parts_of, first, groups):
    row_ref, w_refs = refs[0], refs[1 : 1 + sum(parts_of)]
    out_ref, row_held, total, out_held, w_held, sems = refs[-6:]
    count, out_width = out_held.shape
    width = row_ref.shape[2]
    row_copy = pltpu.make_async_copy(row_ref, row_held, sems.at[len(w_refs)])
    row_copy.start()
    copies, places = [], []
    for turn, parts in enumerate(parts_of):
        source, size = place_ref[0] ^ turn, width // parts
        for part in range(parts):
            at, row = len(copies), turn * width + part * size
            copies.append(pltpu.make_async_copy(w_refs[at], w_held.at[row : row + size], sems.at[at]))
            place = part if parts == 1 else place_ref[1] ^ part
            places.append((turn, source, pl.ds(pl.multiple_of(place * size, size), size)))
    step = len(parts_of) // groups
    strip = out_width // groups

    def fetch(group):
        for copy, (turn, _, _) in zip(copies, places):
            if turn // step == group:
                copy.start()

    ahead = 3
    for group in range(min(ahead, groups)):
        fetch(group)
    row_copy.wait()
    sends = []
    for group in range(groups):
        found = []
        for copy, (turn, source, cols) in zip(copies, places):
            if turn // step == group:
                copy.wait()
                found.append(row_held[source, :, cols])
        if group + ahead < groups:
            fetch(group + ahead)
        rows = jnp.concatenate(found, axis=1)
        met = slice(group * step * width, (group + 1) * step * width)
        for at in range(groups):
            cols = slice(at * strip, (at + 1) * strip)
            term = jnp.dot(rows, w_held[met, cols], preferred_element_type=F32)
            if group > 0:
                term = total[:, cols] + term
            if group < groups - 1:
                total[:, cols] = term
            else:
                out_held[:, cols] = term.astype(BF16)
                sends.append(
                    pltpu.make_async_copy(
                        out_held.at[:, cols],
                        out_ref.at[first : first + count, cols],
                        sems.at[len(w_refs) + 1 + at],
                    )
                )
                sends[-1].start()
    for send in sends:
        send.wait()


def project(place, chunk, pieces, first, tokens, so_far=None):
    sources, count, width = chunk.shape
    flat = [part for piece in pieces for part in piece]
    depth, out_width = width * sources, flat[0].shape[1]
    groups = 4 if sources % 4 == 0 and out_width % 512 == 0 else 1
    extra = () if so_far is None else (so_far,)
    operands = (chunk, *flat, *extra)
    anywhere = pl.BlockSpec(memory_space=pl.ANY)
    return pl.pallas_call(
        functools.partial(
            project_body, parts_of=tuple(map(len, pieces)), first=first, groups=groups
        ),
        name="project",
        out_shape=jax.ShapeDtypeStruct((tokens, out_width), BF16),
        grid_spec=pltpu.PrefetchScalarGridSpec(
            num_scalar_prefetch=1,
            grid=(1,),
            in_specs=[anywhere] * len(operands),
            out_specs=anywhere,
            scratch_shapes=[
                pltpu.VMEM(chunk.shape, BF16),
                pltpu.VMEM((count, out_width), F32),
                pltpu.VMEM((count, out_width), BF16),
                pltpu.VMEM((depth, out_width), BF16),
                pltpu.SemaphoreType.DMA((len(flat) + 1 + groups,)),
            ],
        ),
        input_output_aliases={} if so_far is None else {len(operands): 0},
        compiler_params=pltpu.CompilerParams(vmem_limit_bytes=PROJECT_VMEM),
        cost_estimate=pl.CostEstimate(
            flops=2 * count * depth * out_width,
            bytes_accessed=2 * (count * depth + depth * out_width + count * out_width),
            transcendentals=0,
        ),
    )(place, *operands)


def per_device(
    sizes, query, keys, values, mem_init, beta, mem_gain, loc_gain, w_out
):
    seq_size, head_size = sizes
    tokens, width = query.shape
    dests = head_size * SEG // tokens
    per_dest = SEG // dests
    me, now = lax.axis_index("head"), lax.axis_index("seq")
    place = jnp.stack([me, now % 2]).astype(jnp.int32)
    mem_gain, loc_gain = mem_gain.reshape(1, width), loc_gain.reshape(1, width)

    gather = RowGather(w_out, seq_size, head_size)
    gather.near()
    terms, total = kv_terms(keys, values)
    totals = [
        lax.ppermute(total, "seq", [(at, at + step) for at in range(seq_size - step)])
        for step in range(1, seq_size)
    ]

    groups = [(0, per_dest // 2), (per_dest // 2, per_dest // 2)]
    *near, last = range(2, head_size, 2)
    arrays = (query, keys, values, mem_init, terms, beta, mem_gain, loc_gain)
    arrived, after = [], ()
    for block in groups:
        first = block == groups[0]
        chunk, prefix = chunk_call(block, dests, arrays, totals, after, 0.01 if first else 20)
        if first:
            memory_prefix = prefix
            after = gather.now(*near, last)
        else:
            for turn in near:
                gather.swap(turn)
            chunk, early = lax.optimization_barrier((chunk, [gather.pieces[turn] for turn in near]))
            gather.pieces.update(zip(near, early))
            _, held = lax.optimization_barrier((chunk, gather.pieces[last]))
            gather.pieces[last] = held
            gather.swap(last)
            for turn in (0, *near, last):
                gather.across(turn)
        arrived.append(lax.all_to_all(chunk, "head", split_axis=0, concat_axis=0, tiled=True))
    pieces = gather.all()
    out = None
    for (start, _), chunk in zip(groups, arrived):
        out = project(place, chunk, pieces, start, tokens // head_size, out)
    return out, memory_prefix


def solution(mesh):
    sizes = (mesh.shape["seq"], mesh.shape["head"])
    in_specs = (
        P("seq", "head"),
        P("seq", "head"),
        P("seq", "head"),
        P("head", None, None),
        P("head"),
        P("head"),
        P("head"),
        P("head", None),
    )
    out_specs = (P(("seq", "head"), None), P("seq", "head", None, None))
    return jax.shard_map(
        functools.partial(per_device, sizes),
        mesh=mesh,
        in_specs=in_specs,
        out_specs=out_specs,
        check_vma=False,
    )
```
